256 devices in a mesh: layer: 4 (over y), perm: 8 (over z), owner: 8 (over x, core).
Axes of the slice: x: 4, y: 4, z: 8, core: 2. Of those that a mesh axis runs over, the one named last changes fastest.
Arguments:
- amplitudes: bfloat16 [1024, 32768], P(('layer', 'perm'), 'owner'), may hold values from -6 to 6
- integrals: bfloat16 [32768, 16384], P(('layer', 'perm'), 'owner'), may hold values from -0.125 to 0.125
- contract_irrep: int32 [256], replicated, may hold values from 0 to 3
- output_irrep: int32 [128], replicated, may hold values from 0 to 3
- occ_energy: float32 [1024], P(('layer', 'perm')), may hold values from -4 to -0.5
- virt_energy: float32 [16384], P('owner'), may hold values from 0.5 to 4
Outputs:
- ladder_update: float32 [1024, 16384], P(('layer', 'perm'), 'owner')
The draws below stay inside these ranges and needn't reach their ends.
All inputs are finite; a program needn't handle non-finite values.
Results may differ from the reference program's by a relative error of at most 0.0003.
Values may be sent and summed in bfloat16 or wider, within the bound.
A program may use at most 64 MiB of HBM per device.

```python
import math
import jax
import jax.numpy as jnp
import numpy as np
from jax import lax

BW = 128
NIRREP = 4
NB_DEV = 16
PAIRS = 1024
KB = 256
NB = 128
KC = 32768
NAB = 16384


def with_ends(values, key, least, high):
    spot = [jax.random.randint(jax.random.fold_in(key, axis), (), 0, length) for axis, length in enumerate(values.shape)]
    longest = values.shape.index(max(values.shape))
    neighbour = spot[:longest] + [(spot[longest] + 1) % values.shape[longest]] + spot[longest + 1:]
    return values.at[tuple(spot)].set(least).at[tuple(neighbour)].set(high)


def block_levels(stream_key, dims, pieces, smallest, top_value):
    def one(position, parts):
        heights = jax.random.uniform(jax.random.fold_in(jax.random.fold_in(stream_key, 6), position), (parts,), jnp.float32, smallest / len(pieces), top_value / len(pieces))
        return jnp.repeat(jnp.exp(heights), dims[position] // parts).reshape((-1,) + (1,) * (len(dims) - position - 1))

    factor_of = one(*pieces[0])
    for cut in pieces[1:]:
        factor_of = factor_of * one(*cut)
    return factor_of


def cumulative_ranks(count, skew):
    loads = [(1 << 20) // math.isqrt(grade ** skew) + 1 for grade in range(1, count + 1)]
    deviation = 1 + sum(loads) // (1 << 30)
    return np.cumsum(np.array([max(1, weight // deviation) for weight in loads]))


def ranked(rng, shape, amount, skew):
    grid = cumulative_ranks(amount, skew)
    lot = jax.random.randint(jax.random.fold_in(rng, 1), shape, 0, int(grid[amount - 1]))
    grade = jnp.searchsorted(jnp.asarray(grid, jnp.int32), lot, side="right")
    return jax.random.permutation(jax.random.fold_in(rng, 2), amount)[grade].astype(jnp.int32)


def noise(key, dims, deviation, bound, pieces=(), kind=jnp.bfloat16):
    result = jax.random.normal(key, dims, jnp.float32) * deviation
    if len(pieces) > 0:
        result = block_levels(key, dims, pieces, -0.22, 0.18) * result
    return jnp.clip(result, min=-bound, max=bound).astype(kind)


def setup_inputs(seed: int = 0) -> dict:
    keys = jax.random.split(jax.random.key(seed), 7)
    amplitudes = noise(keys[0], (PAIRS, KC), 1.0, 6.0, ((0, 32), (1, 8)))
    integrals = noise(keys[1], (KC, NAB), (KC // 16) ** -0.5, 0.125, ((0, 32), (1, 8)))
    contract_irrep = with_ends(ranked(keys[2], (KB,), NIRREP, 2), jax.random.fold_in(keys[2], 3), 0, NIRREP - 1).astype(jnp.int32)
    output_irrep = with_ends(ranked(keys[3], (NB,), NIRREP, 1), jax.random.fold_in(keys[3], 3), 0, NIRREP - 1).astype(jnp.int32)
    occ_energy = jnp.clip(-4.0 + 3.5 * jax.random.uniform(keys[4], (PAIRS,), jnp.float32) ** block_levels(keys[4], (PAIRS,), ((0, 32),), -0.2, 0.2), -4.0, -0.5)
    virt_energy = jnp.clip(0.5 + 3.5 * jax.random.uniform(keys[5], (NAB,), jnp.float32) ** block_levels(keys[5], (NAB,), ((0, 8),), -0.2, 0.2), 0.5, 4.0)
    return {"amplitudes": amplitudes, "integrals": integrals, "contract_irrep": contract_irrep, "output_irrep": output_irrep, "occ_energy": occ_energy, "virt_energy": virt_energy}


def reference(amplitudes, integrals, contract_irrep, output_irrep, occ_energy, virt_energy):
    column_width = NB_DEV * BW
    block_total = NAB // column_width
    row_irrep = jnp.repeat(contract_irrep, BW, total_repeat_length=KC)
    column_irrep_all = jnp.repeat(output_irrep, BW, total_repeat_length=NAB)

    def one_block(index):
        begin_col = (index * column_width).astype(jnp.int32)
        columns = lax.dynamic_slice_in_dim(integrals, begin_col, column_width, 1)
        column_irrep = lax.dynamic_slice_in_dim(column_irrep_all, begin_col, column_width, 0)
        energies = lax.dynamic_slice_in_dim(virt_energy, begin_col, column_width, 0)
        matching = row_irrep[:, None] == column_irrep[None, :]
        sector = jnp.where(matching, columns, jnp.zeros_like(columns))
        ladder = jnp.dot(amplitudes, sector, preferred_element_type=jnp.float32)
        return ladder / (energies[None, :] - occ_energy[:, None])

    blocks = lax.map(one_block, jnp.arange(block_total, dtype=jnp.int32))
    return jnp.transpose(blocks, (1, 0, 2)).reshape(PAIRS, NAB)
```

```python
import functools

import jax
import jax.numpy as jnp
from jax import lax
from jax.experimental import pallas as pl
from jax.experimental.pallas import tpu as pltpu
from jax.sharding import PartitionSpec as P

BW = 128
LANES = 128
CHUNK = 32
PIECE = 256
NY = 5
TOP = 32767.0
MESH = pl.DeviceIdType.MESH


class Ring:
    def __init__(self, axis, n, groups, own, bufs):
        self.axis, self.n, self.groups, self.own = axis, n, groups, own
        self.sq, self.rq, self.ss, self.rs, self.sems = bufs
        self.me = lax.axis_index(axis)

    def copies(self, p, t, d):
        where = {self.axis: lax.rem(self.me + (1 if d == 0 else self.n - 1), self.n)}
        at = (p, t, d, d) if t == 0 else (p, t, d)
        return [
            pltpu.make_async_remote_copy(
                src_ref=self.sq.at[at],
                dst_ref=self.rq.at[at],
                send_sem=self.sems.at[0, p, t, d],
                recv_sem=self.sems.at[1, p, t, d],
                device_id=where,
                device_id_type=MESH,
            ),
            pltpu.make_async_remote_copy(
                src_ref=self.ss.at[p, t, d],
                dst_ref=self.rs.at[p, t, d],
                send_sem=self.sems.at[2, p, t, d],
                recv_sem=self.sems.at[3, p, t, d],
                device_id=where,
                device_id_type=MESH,
            ),
        ]

    def each_group(self, body):
        if self.groups == 1:
            body(0)
        else:
            def step(g, carry):
                body(g)
                return carry

            lax.fori_loop(0, self.groups, step, 0, unroll=2)

    def rows(self, g):
        return pl.ds(g * CHUNK if isinstance(g, int) else pl.multiple_of(g * CHUNK, CHUNK), CHUNK)

    def decode(self, p, t, d, h, g):
        coded = self.rq[p, t, d, h, self.rows(g), :].astype(jnp.int32).astype(jnp.float32)
        return coded * self.rs[p, t, d, pl.ds(g, 1), :]

    def wait(self, p, t, d):
        for copy in self.copies(p, t, d):
            copy.wait_recv()

    def send(self, p, t):
        half = self.n // 2
        for d in range(2):
            dest = lax.rem(self.me + (half - t if d == 0 else half + t), self.n)
            if t > 0:
                self.wait(p, t - 1, d)

            def body(g, d=d, dest=dest):
                halves = (d,) if t == 0 else (0, 1)
                values = []
                for h in halves:
                    value = self.own(p, dest, g, h)
                    if t > 1 or (t == 1 and h == d):
                        value = value + self.decode(p, t - 1, d, h, g)
                    values.append(value)
                most = jnp.max(functools.reduce(jnp.maximum, [jnp.abs(v) for v in values]), axis=0, keepdims=True)
                scale = jnp.maximum(most, 1e-30) * (1.0 / TOP)
                factor = 1.0 / scale
                self.ss[p, t, d, pl.ds(g, 1), :] = scale
                for h, value in zip(halves, values):
                    coded = jnp.round(value * factor).astype(jnp.int32).astype(jnp.int16)
                    self.sq[p, t, d, h, self.rows(g), :] = coded

            self.each_group(body)
            for copy in self.copies(p, t, d):
                copy.start()

    def final(self, p, store):
        last = self.n // 2 - 1
        for d in range(2):
            self.wait(p, last, d)

        def body(g):
            for h in range(2):
                total = self.own(p, self.me, g, h) + self.decode(p, last, 0, h, g)
                store(p, g, h, total + self.decode(p, last, 1, h, g))

        self.each_group(body)

    def drain(self, pieces):
        def step(p, carry):
            for t in range(self.n // 2):
                for d in range(2):
                    for copy in self.copies(p, t, d):
                        copy.wait_send()
            return carry

        lax.fori_loop(0, pieces, step, 0)


def kernel(ny, nz, nx, cirr, oirr, amp, integ, out, abuf, im, part, qy, qz, asems, *ring_bufs):
    y, z, o = lax.axis_index("layer"), lax.axis_index("perm"), lax.axis_index("owner")
    x, c = o // 2, lax.rem(o, 2)
    pieces = im.shape[1] // PIECE
    n_z = pieces - NY
    depth = im.shape[0]
    per_core = nz // 2
    groups = nz // 2
    s1_send, s1_recv, x_send, x_recv, y_send, y_recv, b_send, b_recv, i_sem = asems

    barrier = pltpu.get_barrier_semaphore()
    for k in range(1, nz):
        pl.semaphore_signal(barrier, inc=1, device_id={"perm": lax.rem(z + k, nz)}, device_id_type=MESH)
    for k in range(1, ny):
        pl.semaphore_signal(barrier, inc=1, device_id={"layer": lax.rem(y + k, ny)}, device_id_type=MESH)
    for k in range(1, nx):
        pl.semaphore_signal(barrier, inc=1, device_id={"owner": lax.rem(o + 2 * k, 2 * nx)}, device_id_type=MESH)
    pl.semaphore_signal(barrier, inc=1, device_id={"owner": o + 1 - 2 * c}, device_id_type=MESH)

    load = [
        pltpu.make_async_copy(integ.at[pl.ds(k * BW, BW)], im.at[pl.ds(k * BW, BW)], i_sem.at[k])
        for k in range(depth // BW)
    ]
    for copy in load:
        copy.start()
    pl.semaphore_wait(barrier, nz + ny + nx - 2)

    spare = ny * nz

    def slot(source_x, at_y, zs):
        return jnp.where(source_x == at_y, at_y * nz + zs, spare + source_x * nz + zs)

    def along_z(j):
        return pltpu.make_async_remote_copy(
            src_ref=amp.at[:, pl.ds(j * depth, depth)],
            dst_ref=abuf.at[slot(x, y, z)],
            send_sem=s1_send.at[j],
            recv_sem=s1_recv.at[z],
            device_id={"perm": c * per_core + j},
            device_id_type=MESH,
        )

    for j in range(per_core):
        @pl.when(c * per_core + j != z)
        def _(j=j):
            along_z(j).start()

        @pl.when(c * per_core + j == z)
        def _(j=j):
            pltpu.make_async_copy(amp.at[:, pl.ds(j * depth, depth)], abuf.at[slot(x, y, z)], s1_recv.at[z]).start()

    outer = im.shape[1] // BW
    inner_base = (y * nz + z) * (depth // BW)
    outer_base = o * outer
    for copy in load:
        copy.wait()

    def mask_rows(k, carry):
        row_irrep = cirr[inner_base + k]
        rows = pl.ds(pl.multiple_of(k * BW, BW), BW)
        for b in range(outer):
            cols = pl.ds(b * BW, BW)
            block = im[rows, cols]
            im[rows, cols] = jnp.where(row_irrep == oirr[outer_base + b], block, jnp.zeros_like(block))
        return carry

    lax.fori_loop(0, depth // BW, mask_rows, 0)

    active = c == z // per_core

    def pair(first):
        return abuf.at[pl.ds(first, 2)]

    def along_x(g, k):
        return pltpu.make_async_remote_copy(
            src_ref=pair(slot(x, y, 2 * g)),
            dst_ref=pair(slot(x, y, 2 * g)),
            send_sem=x_send.at[g, k],
            recv_sem=x_recv.at[g, k],
            device_id={"owner": lax.rem(o + 2 * k, 2 * nx)},
            device_id_type=MESH,
        )

    def along_y(g, k, xs):
        return pltpu.make_async_remote_copy(
            src_ref=pair(spare + xs * nz + 2 * g),
            dst_ref=pair(y * nz + 2 * g),
            send_sem=y_send.at[g, k],
            recv_sem=y_recv.at[g, y],
            device_id={"layer": xs},
            device_id_type=MESH,
        )

    def from_y(g, ys):
        return pltpu.make_async_remote_copy(
            src_ref=pair(ys * nz + 2 * g),
            dst_ref=pair(ys * nz + 2 * g),
            send_sem=y_send.at[g, 0],
            recv_sem=y_recv.at[g, ys],
            device_id={"layer": ys},
            device_id_type=MESH,
        )

    def across(g, ys):
        return pltpu.make_async_remote_copy(
            src_ref=pair(ys * nz + 2 * g),
            dst_ref=pair(ys * nz + 2 * g),
            send_sem=b_send.at[g, ys],
            recv_sem=b_recv.at[g, ys],
            device_id={"owner": o + 1 - 2 * c},
            device_id_type=MESH,
        )

    order = [0, 1, groups - 1] + list(range(2, groups - 1))
    near = [1, 3, 2]

    @pl.when(active)
    def _():
        def hand_on(g, k):
            xs = lax.rem(x + k, nx)

            @pl.when(xs != y)
            def _():
                along_y(g, k, xs).start()

            @pl.when(xs == y)
            def _():
                across(g, y).start()

        for t in order:
            g = lax.rem(z // 2 + t, groups)
            for e in range(2):
                pltpu.make_async_copy(abuf.at[slot(x, y, 2 * g + e)], abuf.at[slot(x, y, 2 * g + e)], s1_recv.at[2 * g + e]).wait()
            for k in near:
                along_x(g, k).start()
            hand_on(g, 0)
        for t in order:
            g = lax.rem(z // 2 + t, groups)
            for k in near:
                xs = lax.rem(x + k, nx)
                pltpu.make_async_copy(pair(slot(xs, y, 2 * g)), pair(slot(xs, y, 2 * g)), x_recv.at[g, nx - k]).wait()
                hand_on(g, k)
        for t in order:
            g = lax.rem(z // 2 + t, groups)
            for k in near:
                ys = lax.rem(y + k, ny)
                from_y(g, ys).wait_recv()
                across(g, ys).start()

    @pl.when(jnp.logical_not(active))
    def _():
        for t in order:
            g = lax.rem(z // 2 + t, groups)
            for ys in range(ny):
                across(g, ys).wait_recv()

    def own_part(base, y_first):
        def own(p, dest, g, h):
            row = (dest * nz + g if y_first else g * nz + dest) * CHUNK
            return part[base + p, h, pl.ds(pl.multiple_of(row, CHUNK), CHUNK), :]
        return own

    def own_sum(ref):
        return lambda p, dest, g, h: ref[p, h, pl.ds(pl.multiple_of(dest * CHUNK, CHUNK), CHUNK), :]

    bufs = [ring_bufs[5 * k: 5 * k + 5] for k in range(4)]
    y1 = Ring("layer", ny, nz, own_part(0, True), bufs[0])
    z2 = Ring("perm", nz, 1, own_sum(qy), bufs[1])
    z1 = Ring("perm", nz, ny, own_part(NY, False), bufs[2])
    y2 = Ring("layer", ny, 1, own_sum(qz), bufs[3])

    def multiply(piece):
        cols = pl.ds(pl.multiple_of(piece * PIECE, PIECE), PIECE)
        block = im[:, cols]
        tall = 512

        def body(r, carry):
            rows = abuf[pl.ds(r * (tall // CHUNK), tall // CHUNK)].reshape(tall, depth)
            product = jnp.dot(rows, block, preferred_element_type=jnp.float32)
            at = pl.ds(pl.multiple_of(r * tall, tall), tall)
            part[piece, 0, at, :] = product[:, :LANES]
            part[piece, 1, at, :] = product[:, LANES:]
            return carry

        lax.fori_loop(0, ny * nz * CHUNK // tall, body, 0)

    def store_sum(ref):
        def store(p, g, h, value):
            ref[p, h, pl.ds(g * CHUNK if isinstance(g, int) else pl.multiple_of(g * CHUNK, CHUNK), CHUNK), :] = value
        return store

    def store_out(base):
        def store(p, g, h, value):
            out[:, pl.ds(pl.multiple_of((base + p) * PIECE + h * LANES, LANES), LANES)] = value
        return store

    def y_start(p):
        multiply(p)
        y1.send(p, 0)

    def y_turn(p):
        y1.final(p, store_sum(qy))
        z2.send(p, 0)

    def z_start(p):
        multiply(NY + p)
        z1.send(p, 0)

    def z_turn(p):
        z1.final(p, store_sum(qz))
        y2.send(p, 0)

    y_stages = [y_start, lambda p: y1.send(p, 1), y_turn] + [functools.partial(lambda t, p: z2.send(p, t), t) for t in (1, 2, 3)]
    y_stages += [lambda p: z2.final(p, store_out(0))]
    z_stages = [z_start] + [functools.partial(lambda t, p: z1.send(p, t), t) for t in (1, 2, 3)]
    z_stages += [z_turn, lambda p: y2.send(p, 1), lambda p: y2.final(p, store_out(NY))]

    def tick(k, carry):
        for s in range(len(y_stages)):
            @pl.when((k >= s) & (k - s < NY))
            def _(s=s):
                y_stages[s](k - s)

            @pl.when((k >= s) & (k - s < n_z))
            def _(s=s):
                z_stages[s](k - s)
        return carry

    lax.fori_loop(0, NY + len(y_stages) - 1, tick, 0)

    for j in range(per_core):
        @pl.when(c * per_core + j != z)
        def _(j=j):
            along_z(j).wait_send()

    @pl.when(active)
    def _():
        for g in range(groups):
            for k in near:
                along_x(g, k).wait_send()
            for k in range(nx):
                xs = lax.rem(x + k, nx)

                @pl.when(xs != y)
                def _(g=g, k=k, xs=xs):
                    along_y(g, k, xs).wait_send()
            for ys in range(ny):
                across(g, ys).wait_send()

    y1.drain(NY)
    z2.drain(NY)
    z1.drain(n_z)
    y2.drain(n_z)


def solution(mesh):
    ny, nz, nx = mesh.shape["layer"], mesh.shape["perm"], mesh.shape["owner"] // 2

    def local(amplitudes, integrals, contract_irrep, output_irrep, occ_energy, virt_energy):
        rows = amplitudes.shape[0]
        depth, width = integrals.shape
        pieces = width // PIECE
        n_z = pieces - NY
        groups = nz // 2
        dma = pltpu.SemaphoreType.DMA
        rings = []
        for n, count, size in ((ny, NY, nz), (nz, NY, 1), (nz, n_z, ny), (ny, n_z, 1)):
            rings += [pltpu.VMEM((count, n // 2, 2, 2, size * CHUNK, LANES), jnp.int16)] * 2
            rings += [pltpu.VMEM((count, n // 2, 2, size, LANES), jnp.float32)] * 2
            rings += [dma((4, count, n // 2, 2))]
        asems = (
            dma((nz // 2,)), dma((nz,)),
            dma((groups, nx)), dma((groups, nx)),
            dma((groups, nx)), dma((groups, ny)),
            dma((groups, ny)), dma((groups, ny)),
            dma((depth // BW,)),
        )
        ladder = pl.pallas_call(
            functools.partial(kernel, ny, nz, nx),
            out_shape=jax.ShapeDtypeStruct((rows, width), jnp.float32),
            in_specs=[pl.BlockSpec(memory_space=pltpu.SMEM)] * 2
            + [pl.BlockSpec(memory_space=pltpu.VMEM), pl.BlockSpec(memory_space=pl.ANY)],
            out_specs=pl.BlockSpec(memory_space=pltpu.VMEM),
            scratch_shapes=[
                pltpu.VMEM((2 * ny * nz, rows, depth), jnp.bfloat16),
                pltpu.VMEM((depth, width), jnp.bfloat16),
                pltpu.VMEM((pieces, 2, ny * nz * CHUNK, LANES), jnp.float32),
                pltpu.VMEM((NY, 2, nz * CHUNK, LANES), jnp.float32),
                pltpu.VMEM((n_z, 2, ny * CHUNK, LANES), jnp.float32),
                asems,
            ] + rings,
            compiler_params=pltpu.CompilerParams(
                collective_id=0, has_side_effects=True, vmem_limit_bytes=56 * 2**20
            ),
            cost_estimate=pl.CostEstimate(
                flops=2 * ny * nz * rows * depth * width, bytes_accessed=2 * depth * width, transcendentals=0
            ),
        )(contract_irrep, output_irrep, amplitudes, integrals)
        return ladder / (virt_energy[None, :] - occ_energy[:, None])

    return jax.shard_map(
        local,
        mesh=mesh,
        in_specs=(
            P(("layer", "perm"), "owner"),
            P(("layer", "perm"), "owner"),
            P(),
            P(),
            P(("layer", "perm")),
            P("owner"),
        ),
        out_specs=P(("layer", "perm"), "owner"),
        check_vma=False,
    )
```

```python
import functools

import jax
import jax.numpy as jnp
from jax import lax
from jax.experimental import pallas as pl
from jax.experimental.pallas import tpu as pltpu
from jax.sharding import PartitionSpec as P

BW = 128
LANES = 128
CHUNK = 32
PIECE = 256
TOP = 32767.0
MESH = pl.DeviceIdType.MESH

Y_GROUPS = ((0, 3), (3, 2))
Z_GROUPS = ((0, 1), (1, 1), (2, 1))
Z_ALL = ((0, 3),)
NY, NZ = 5, 3


class Ring:
    def __init__(self, axis, n, slots, groups, own, bufs):
        self.axis, self.n, self.slots, self.groups, self.own = axis, n, slots, groups, own
        self.sq, self.rq, self.ss, self.rs, self.sems = bufs
        self.me = lax.axis_index(axis)

    def copies(self, v, t, d, g):
        where = {self.axis: lax.rem(self.me + (1 if d == 0 else self.n - 1), self.n)}
        first, count = self.groups[g]
        rows, pieces = pl.ds(0, self.slots[v]), pl.ds(first, count)
        at = (v, t, d, rows, pieces, d) if t == 0 else (v, t, d, rows, pieces)
        scales = (v, t, d, rows, pieces)
        return [
            pltpu.make_async_remote_copy(
                src_ref=self.sq.at[at],
                dst_ref=self.rq.at[at],
                send_sem=self.sems.at[0, v, t, d, g],
                recv_sem=self.sems.at[1, v, t, d, g],
                device_id=where,
                device_id_type=MESH,
            ),
            pltpu.make_async_remote_copy(
                src_ref=self.ss.at[scales],
                dst_ref=self.rs.at[scales],
                send_sem=self.sems.at[2, v, t, d, g],
                recv_sem=self.sems.at[3, v, t, d, g],
                device_id=where,
                device_id_type=MESH,
            ),
        ]

    def each(self, v, g, body):
        first, count = self.groups[g]
        total = self.slots[v] * count

        def step(k, carry):
            body(k // count, first + lax.rem(k, count))
            return carry

        lax.fori_loop(0, total, step, 0, unroll=2 if total % 2 == 0 else 1)

    def decode(self, v, t, d, s, p, h):
        return self.rq[v, t, d, s, p, h].astype(jnp.int32).astype(jnp.float32) * self.rs[v, t, d, s, p]

    def wait(self, v, t, d, g):
        for copy in self.copies(v, t, d, g):
            copy.wait_recv()

    def send(self, v, t, g):
        for d in range(2):
            if t > 0:
                self.wait(v, t - 1, d, g)

            def body(s, p, d=d):
                halves = (d,) if t == 0 else (0, 1)
                values = []
                for h in halves:
                    value = self.own(v, t, d, s, p, h)
                    if t > 1 or (t == 1 and h == d):
                        value = value + self.decode(v, t - 1, d, s, p, h)
                    values.append(value)
                most = jnp.max(functools.reduce(jnp.maximum, [jnp.abs(u) for u in values]), axis=0, keepdims=True)
                scale = jnp.maximum(most, 1e-30) * (1.0 / TOP)
                factor = 1.0 / scale
                self.ss[v, t, d, s, p] = scale
                for h, value in zip(halves, values):
                    self.sq[v, t, d, s, p, h] = jnp.round(value * factor).astype(jnp.int32).astype(jnp.int16)

            self.each(v, g, body)
            for copy in self.copies(v, t, d, g):
                copy.start()

    def final(self, v, g, store):
        last = self.n // 2 - 1
        for d in range(2):
            self.wait(v, last, d, g)

        def body(s, p):
            for h in range(2):
                total = self.own(v, None, None, s, p, h) + self.decode(v, last, 0, s, p, h)
                store(s, p, h, total + self.decode(v, last, 1, s, p, h))

        self.each(v, g, body)

    def drain(self):
        for v in range(len(self.slots)):
            for t in range(self.n // 2):
                for d in range(2):
                    for g in range(len(self.groups)):
                        for copy in self.copies(v, t, d, g):
                            copy.wait_send()


def kernel(ny, nz, nx, cirr, oirr, amp, integ, out, abuf, im, part, qy, qz, asems, *ring_bufs):
    y, z, o = lax.axis_index("layer"), lax.axis_index("perm"), lax.axis_index("owner")
    x, c = o // 2, lax.rem(o, 2)
    depth, width = im.shape
    half = nz // 2
    a_send, a_recv, x_send, x_recv, b_send, b_recv, i_sem = asems
    active = c == z // half
    sibling = {"owner": o + 1 - 2 * c}

    def row_of(column, zs, at_z):
        return lax.rem(column + 4 * nx - zs - at_z, nx)

    barrier = pltpu.get_barrier_semaphore()

    def greet(where):
        pl.semaphore_signal(barrier, inc=1, device_id=where, device_id_type=MESH)

    for k in (1, nz - 1):
        greet({"perm": lax.rem(z + k, nz)})
    for k in (1, ny - 1):
        greet({"layer": lax.rem(y + k, ny)})
    for k in range(1, nx):
        greet({"owner": lax.rem(o + 2 * k, 2 * nx)})
    greet(sibling)
    for zs in range(nz):
        ys = row_of(x, zs, z)

        @pl.when(active & jnp.logical_not((x == y) & (ys == y) & (z == zs)))
        def _(zs=zs, ys=ys):
            greet({"owner": 2 * y + c, "layer": ys, "perm": jnp.int32(zs)})

    load = [
        pltpu.make_async_copy(integ.at[pl.ds(k * BW, BW)], im.at[pl.ds(k * BW, BW)], i_sem.at[k])
        for k in range(depth // BW)
    ]
    for copy in load:
        copy.start()

    def block(k):
        j = lax.rem(z + jnp.where(active, (2, 1, 3, 0)[k], (0, 1, 3, 2)[k]), half)
        to_z = half * c + j
        column = lax.rem(y + z + to_z, nx)
        mine = (column == x) & (x == y) & (to_z == z)
        source = amp.at[:, pl.ds(pl.multiple_of(j * depth, depth), depth)]
        remote = pltpu.make_async_remote_copy(
            src_ref=source,
            dst_ref=abuf.at[z, y],
            send_sem=a_send.at[k],
            recv_sem=a_recv.at[z],
            device_id={"owner": 2 * column + c, "layer": x, "perm": to_z},
            device_id_type=MESH,
        )
        return mine, remote, pltpu.make_async_copy(source, abuf.at[z, y], a_recv.at[z])

    keeps = active & (x == y) & (lax.rem(y + 2 * z, nx) == x)
    pl.semaphore_wait(barrier, nx + 4 + half - keeps.astype(jnp.int32))
    for k in range(half):
        mine, remote, here = block(k)

        @pl.when(jnp.logical_not(mine))
        def _(remote=remote):
            remote.start()

        @pl.when(mine)
        def _(here=here):
            here.start()

    outer = width // BW
    inner_base = (y * nz + z) * (depth // BW)
    outer_base = o * outer
    for copy in load:
        copy.wait()

    def mask_rows(k, carry):
        row_irrep = cirr[inner_base + k]
        rows = pl.ds(pl.multiple_of(k * BW, BW), BW)
        for b in range(outer):
            cols = pl.ds(b * BW, BW)
            values = im[rows, cols]
            im[rows, cols] = jnp.where(row_irrep == oirr[outer_base + b], values, jnp.zeros_like(values))
        return carry

    lax.fori_loop(0, depth // BW, mask_rows, 0)

    def places(u):
        if u == 0:
            return [lax.rem(z + half, nz)]
        if u == half:
            return [z]
        return [lax.rem(z + half - u, nz), lax.rem(z + half + u, nz)]

    def along_x(zs, k):
        ys = row_of(x, zs, z)
        return pltpu.make_async_remote_copy(
            src_ref=abuf.at[zs, ys],
            dst_ref=abuf.at[zs, ys],
            send_sem=x_send.at[zs, k],
            recv_sem=x_recv.at[zs, k],
            device_id={"owner": lax.rem(o + 2 * k, 2 * nx)},
            device_id_type=MESH,
        )

    def across(zs):
        return pltpu.make_async_remote_copy(
            src_ref=abuf.at[zs],
            dst_ref=abuf.at[zs],
            send_sem=b_send.at[zs],
            recv_sem=b_recv.at[zs],
            device_id=sibling,
            device_id_type=MESH,
        )

    def spread(u):
        if u > half:
            return

        @pl.when(active)
        def _():
            for zs in places(u):
                ys = row_of(x, zs, z)
                pltpu.make_async_copy(abuf.at[zs, ys], abuf.at[zs, ys], a_recv.at[zs]).wait()
                for k in range(1, nx):
                    along_x(zs, k).start()

    def collect(u):
        if u > half:
            return

        @pl.when(active)
        def _():
            for zs in places(u):
                for k in range(1, nx):
                    ys = row_of(lax.rem(x + nx - k, nx), zs, z)
                    pltpu.make_async_copy(abuf.at[zs, ys], abuf.at[zs, ys], x_recv.at[zs, k]).wait()
                across(zs).start()

    def arrive(u):
        @pl.when(jnp.logical_not(active))
        def _():
            for zs in places(u):
                across(zs).wait_recv()

    tall = ny * CHUNK

    def multiply(u, first, count):
        def body(k, carry):
            piece = first + k
            right = im[:, pl.ds(pl.multiple_of(piece * PIECE, PIECE), PIECE)]
            left = [abuf[zs].reshape(tall, depth) for zs in places(u)]
            product = jnp.dot(jnp.concatenate(left, axis=0), right, preferred_element_type=jnp.float32)
            for k, zs in enumerate(places(u)):
                at = pl.ds(pl.multiple_of(zs * tall, tall), tall)
                part[piece, 0, at, :] = product[k * tall: (k + 1) * tall, :LANES]
                part[piece, 1, at, :] = product[k * tall: (k + 1) * tall, LANES:]
            return carry

        lax.fori_loop(0, count, body, 0)

    def toward(me, n, t, d):
        if t is None:
            return me
        return lax.rem(me + (n // 2 - t if d == 0 else n // 2 + t), n)

    def rows_at(piece, h, at_z, at_y):
        return part[piece, h, pl.ds(pl.multiple_of((at_z * ny + at_y) * CHUNK, CHUNK), CHUNK), :]

    def y1_own(v, t, d, s, p, h):
        where = places(v)
        at_z = where[0] if len(where) == 1 else jnp.where(s == 0, where[0], where[1])
        return rows_at(p, h, at_z, toward(y, ny, t, d))

    def z1_own(v, t, d, s, p, h):
        return rows_at(NY + p, h, toward(z, nz, t, d), s)

    def z2_own(v, t, d, s, p, h):
        return qy[nz - 1 if t is None else 0 if t == 0 else 2 * t - 1 + d, p, h]

    def y2_own(v, t, d, s, p, h):
        return qz[toward(y, ny, t, d), p, h]

    bufs = [ring_bufs[5 * k: 5 * k + 5] for k in range(4)]
    y1 = Ring("layer", ny, [len(places(u)) for u in range(half + 1)], Y_GROUPS, y1_own, bufs[0])
    z2 = Ring("perm", nz, [1], Y_GROUPS, z2_own, bufs[1])
    z1 = Ring("perm", nz, [ny], Z_GROUPS, z1_own, bufs[2])
    y2 = Ring("layer", ny, [1], Z_ALL, y2_own, bufs[3])

    def keep_y(u):
        def store(s, p, h, value):
            qy[max(2 * u - 1, 0) + s, p, h] = value
        return store

    def keep_z(s, p, h, value):
        qz[s, p, h] = value

    def write(base):
        def store(s, p, h, value):
            out[:, pl.ds(pl.multiple_of((base + p) * PIECE + h * LANES, LANES), LANES)] = value
        return store

    spread(0)
    spread(1)
    collect(0)
    for i in range(half + 3):
        if i <= half:
            spread(i + 2)
            arrive(i)
            for g, (first, count) in enumerate(Y_GROUPS):
                multiply(i, first, count)
                y1.send(i, 0, g)
        if 1 <= i <= half + 1:
            for g in range(len(Y_GROUPS)):
                y1.send(i - 1, 1, g)
        if i <= half:
            for g, (first, count) in enumerate(Z_GROUPS):
                multiply(i, NY + first, count)
                if i < half:
                    z1.send(0, i, g)
                else:
                    z1.final(0, g, keep_z)
            collect(i + 1)
        if i == half:
            y2.send(0, 0, 0)
        if i == half + 1:
            y2.send(0, 1, 0)
        if i == half + 2:
            y2.final(0, 0, write(NY))
        if i >= 2:
            u = i - 2
            for g in range(len(Y_GROUPS)):
                y1.final(u, g, keep_y(u))
                if u < half:
                    z2.send(0, u, g)
                else:
                    z2.final(0, g, write(0))

    for k in range(half):
        mine, remote, here = block(k)

        @pl.when(jnp.logical_not(mine))
        def _(remote=remote):
            remote.wait_send()

    @pl.when(active)
    def _():
        for zs in range(nz):
            for k in range(1, nx):
                along_x(zs, k).wait_send()
            across(zs).wait_send()

    for ring in (y1, z2, z1, y2):
        ring.drain()


def solution(mesh):
    ny, nz, nx = mesh.shape["layer"], mesh.shape["perm"], mesh.shape["owner"] // 2

    def local(amplitudes, integrals, contract_irrep, output_irrep, occ_energy, virt_energy):
        rows = amplitudes.shape[0]
        depth, width = integrals.shape
        dma = pltpu.SemaphoreType.DMA
        rings = []
        for n, turns, slots, pieces, groups in (
            (ny, nz // 2 + 1, 2, NY, len(Y_GROUPS)),
            (nz, 1, 1, NY, len(Y_GROUPS)),
            (nz, 1, ny, NZ, len(Z_GROUPS)),
            (ny, 1, 1, NZ, len(Z_ALL)),
        ):
            rings += [pltpu.VMEM((turns, n // 2, 2, slots, pieces, 2, CHUNK, LANES), jnp.int16)] * 2
            rings += [pltpu.VMEM((turns, n // 2, 2, slots, pieces, 1, LANES), jnp.float32)] * 2
            rings += [dma((4, turns, n // 2, 2, groups))]
        asems = (
            dma((nz // 2,)), dma((nz,)),
            dma((nz, nx)), dma((nz, nx)),
            dma((nz,)), dma((nz,)),
            dma((depth // BW,)),
        )
        ladder = pl.pallas_call(
            functools.partial(kernel, ny, nz, nx),
            out_shape=jax.ShapeDtypeStruct((rows, width), jnp.float32),
            in_specs=[pl.BlockSpec(memory_space=pltpu.SMEM)] * 2 + [pl.BlockSpec(memory_space=pl.ANY)] * 2,
            out_specs=pl.BlockSpec(memory_space=pltpu.VMEM),
            scratch_shapes=[
                pltpu.VMEM((nz, ny, rows, depth), jnp.bfloat16),
                pltpu.VMEM((depth, width), jnp.bfloat16),
                pltpu.VMEM((NY + NZ, 2, ny * nz * CHUNK, LANES), jnp.float32),
                pltpu.VMEM((nz, NY, 2, CHUNK, LANES), jnp.float32),
                pltpu.VMEM((ny, NZ, 2, CHUNK, LANES), jnp.float32),
                asems,
            ] + rings,
            compiler_params=pltpu.CompilerParams(
                collective_id=0, has_side_effects=True, vmem_limit_bytes=56 * 2**20
            ),
            cost_estimate=pl.CostEstimate(
                flops=2 * ny * nz * rows * depth * width, bytes_accessed=2 * depth * width, transcendentals=0
            ),
        )(contract_irrep, output_irrep, amplitudes, integrals)
        return ladder / (virt_energy[None, :] - occ_energy[:, None])

    return jax.shard_map(
        local,
        mesh=mesh,
        in_specs=(
            P(("layer", "perm"), "owner"),
            P(("layer", "perm"), "owner"),
            P(),
            P(),
            P(("layer", "perm")),
            P("owner"),
        ),
        out_specs=P(("layer", "perm"), "owner"),
        check_vma=False,
    )
```

```python
import functools

import jax
import jax.numpy as jnp
from jax import lax
from jax.experimental import pallas as pl
from jax.experimental.pallas import tpu as pltpu
from jax.sharding import PartitionSpec as P

BW = 128
LANES = 128
CHUNK = 32
PIECE = 256
TOP = 32767.0
MESH = pl.DeviceIdType.MESH

Y_GROUPS = ((0, 3), (3, 2))
Z_GROUPS = ((0, 1), (1, 1), (2, 1))
Z_ALL = ((0, 3),)
NY, NZ = 5, 3


class Ring:
    def __init__(self, axis, n, slots, groups, own, bufs):
        self.axis, self.n, self.slots, self.groups, self.own = axis, n, slots, groups, own
        self.sq, self.rq, self.ss, self.rs, self.sems = bufs
        self.me = lax.axis_index(axis)
        self.started = []

    def copies(self, v, t, d, g):
        where = {self.axis: lax.rem(self.me + (1 if d == 0 else self.n - 1), self.n)}
        first, count = self.groups[g]
        rows, pieces = pl.ds(0, self.slots[v]), pl.ds(first, count)
        at = (v, t, d, rows, pieces, d) if t == 0 else (v, t, d, rows, pieces)
        scales = (v, t, d, rows, pieces)
        return [
            pltpu.make_async_remote_copy(
                src_ref=self.sq.at[at],
                dst_ref=self.rq.at[at],
                send_sem=self.sems.at[0, v, t, d, g],
                recv_sem=self.sems.at[1, v, t, d, g],
                device_id=where,
                device_id_type=MESH,
            ),
            pltpu.make_async_remote_copy(
                src_ref=self.ss.at[scales],
                dst_ref=self.rs.at[scales],
                send_sem=self.sems.at[2, v, t, d, g],
                recv_sem=self.sems.at[3, v, t, d, g],
                device_id=where,
                device_id_type=MESH,
            ),
        ]

    def each(self, v, g, body):
        first, count = self.groups[g]
        total = self.slots[v] * count

        def step(k, carry):
            body(k // count, first + lax.rem(k, count))
            return carry

        lax.fori_loop(0, total, step, 0, unroll=2 if total % 2 == 0 else 1)

    def decode(self, v, t, d, s, p, h):
        return self.rq[v, t, d, s, p, h].astype(jnp.int32).astype(jnp.float32) * self.rs[v, t, d, s, p]

    def wait(self, v, t, d, g):
        for copy in self.copies(v, t, d, g):
            copy.wait_recv()

    def send(self, v, t, g):
        for d in range(2):
            if t > 0:
                self.wait(v, t - 1, d, g)

            def body(s, p, d=d):
                halves = (d,) if t == 0 else (0, 1)
                values = []
                for h in halves:
                    value = self.own(v, t, d, s, p, h)
                    if t > 1 or (t == 1 and h == d):
                        value = value + self.decode(v, t - 1, d, s, p, h)
                    values.append(value)
                most = jnp.max(functools.reduce(jnp.maximum, [jnp.abs(u) for u in values]), axis=0, keepdims=True)
                scale = jnp.maximum(most, 1e-30) * (1.0 / TOP)
                factor = 1.0 / scale
                self.ss[v, t, d, s, p] = scale
                for h, value in zip(halves, values):
                    self.sq[v, t, d, s, p, h] = jnp.round(value * factor).astype(jnp.int32).astype(jnp.int16)

            self.each(v, g, body)
            for copy in self.copies(v, t, d, g):
                copy.start()
        self.started.append((v, t, g))

    def final(self, v, g, store):
        last = self.n // 2 - 1
        for d in range(2):
            self.wait(v, last, d, g)

        def body(s, p):
            for h in range(2):
                total = self.own(v, None, None, s, p, h) + self.decode(v, last, 0, s, p, h)
                store(s, p, h, total + self.decode(v, last, 1, s, p, h))

        self.each(v, g, body)

    def drain(self, keep=0):
        count = max(len(self.started) - keep, 0)
        for v, t, g in self.started[:count]:
            for d in range(2):
                for copy in self.copies(v, t, d, g):
                    copy.wait_send()
        self.started = self.started[count:]


def kernel(ny, nz, nx, cirr, oirr, amp, integ, out, abuf, im, part, qy, qz, asems, *ring_bufs):
    y, z, o = lax.axis_index("layer"), lax.axis_index("perm"), lax.axis_index("owner")
    x, c = o // 2, lax.rem(o, 2)
    depth, width = im.shape
    half = nz // 2
    a_send, a_recv, x_send, x_recv, b_send, b_recv, i_sem = asems
    active = c == z // half
    sibling = {"owner": o + 1 - 2 * c}

    def row_of(column, zs, at_z):
        return lax.rem(column + 4 * nx - zs - at_z, nx)

    barrier = pltpu.get_barrier_semaphore()

    def greet(where):
        pl.semaphore_signal(barrier, inc=1, device_id=where, device_id_type=MESH)

    for zs in range(nz):
        ys = row_of(x, zs, z)

        @pl.when(active & jnp.logical_not((x == y) & (ys == y) & (z == zs)))
        def _(zs=zs, ys=ys):
            greet({"owner": 2 * y + c, "layer": ys, "perm": jnp.int32(zs)})

    for k in (1, nz - 1):
        greet({"perm": lax.rem(z + k, nz)})
    for k in (1, ny - 1):
        greet({"layer": lax.rem(y + k, ny)})
    for k in range(1, nx):
        greet({"owner": lax.rem(o + 2 * k, 2 * nx)})
    greet(sibling)

    load = [
        pltpu.make_async_copy(integ.at[pl.ds(k * BW, BW)], im.at[pl.ds(k * BW, BW)], i_sem.at[k])
        for k in range(depth // BW)
    ]
    for copy in load:
        copy.start()

    orders = (((0, 1, 2, 3), (1, 0, 2, 3), (2, 1, 3, 0), (3, 2, 1, 0)), ((3, 2, 1, 0), (3, 0, 2, 1), (0, 1, 3, 2), (0, 1, 2, 3)))

    def block(k):
        turn = lax.rem(z, half)
        far, near = [
            functools.reduce(lambda rest, r: jnp.where(turn == r, order[r][k], rest), range(1, half), order[0][k])
            for order in orders
        ]
        j = jnp.where(active, near, far)
        to_z = half * c + j
        column = lax.rem(y + z + to_z, nx)
        mine = (column == x) & (x == y) & (to_z == z)
        source = amp.at[:, pl.ds(pl.multiple_of(j * depth, depth), depth)]
        remote = pltpu.make_async_remote_copy(
            src_ref=source,
            dst_ref=abuf.at[z, y],
            send_sem=a_send.at[k],
            recv_sem=a_recv.at[z],
            device_id={"owner": 2 * column + c, "layer": x, "perm": to_z},
            device_id_type=MESH,
        )
        return mine, remote, pltpu.make_async_copy(source, abuf.at[z, y], a_recv.at[z])

    keeps = active & (x == y) & (lax.rem(y + 2 * z, nx) == x)
    pl.semaphore_wait(barrier, nx + 4 + half - keeps.astype(jnp.int32))
    for k in range(half):
        mine, remote, here = block(k)

        @pl.when(jnp.logical_not(mine))
        def _(remote=remote):
            remote.start()

        @pl.when(mine)
        def _(here=here):
            here.start()

    outer = width // BW
    inner_base = (y * nz + z) * (depth // BW)
    outer_base = o * outer
    for copy in load:
        copy.wait()

    def mask_rows(k, carry):
        row_irrep = cirr[inner_base + k]
        rows = pl.ds(pl.multiple_of(k * BW, BW), BW)
        for b in range(outer):
            cols = pl.ds(b * BW, BW)
            values = im[rows, cols]
            im[rows, cols] = jnp.where(row_irrep == oirr[outer_base + b], values, jnp.zeros_like(values))
        return carry

    lax.fori_loop(0, depth // BW, mask_rows, 0)

    def places(u):
        if u == 0:
            return [lax.rem(z + half, nz)]
        if u == half:
            return [z]
        return [lax.rem(z + half - u, nz), lax.rem(z + half + u, nz)]

    def along_x(zs, k):
        ys = row_of(x, zs, z)
        return pltpu.make_async_remote_copy(
            src_ref=abuf.at[zs, ys],
            dst_ref=abuf.at[zs, ys],
            send_sem=x_send.at[zs, k],
            recv_sem=x_recv.at[zs, k],
            device_id={"owner": lax.rem(o + 2 * k, 2 * nx)},
            device_id_type=MESH,
        )

    def across(zs):
        return pltpu.make_async_remote_copy(
            src_ref=abuf.at[zs],
            dst_ref=abuf.at[zs],
            send_sem=b_send.at[zs],
            recv_sem=b_recv.at[zs],
            device_id=sibling,
            device_id_type=MESH,
        )

    def spread(u):
        if u > half:
            return

        @pl.when(active)
        def _():
            for zs in places(u):
                ys = row_of(x, zs, z)
                pltpu.make_async_copy(abuf.at[zs, ys], abuf.at[zs, ys], a_recv.at[zs]).wait()
                for k in range(1, nx):
                    along_x(zs, k).start()

    def collect(u):
        if u > half:
            return

        @pl.when(active)
        def _():
            for zs in places(u):
                for k in range(1, nx):
                    ys = row_of(lax.rem(x + nx - k, nx), zs, z)
                    pltpu.make_async_copy(abuf.at[zs, ys], abuf.at[zs, ys], x_recv.at[zs, k]).wait()
                across(zs).start()

    def arrive(u):
        @pl.when(jnp.logical_not(active))
        def _():
            for zs in places(u):
                across(zs).wait_recv()

    tall = ny * CHUNK

    def multiply(u, first, count):
        def body(k, carry):
            piece = first + k
            right = im[:, pl.ds(pl.multiple_of(piece * PIECE, PIECE), PIECE)]
            left = [abuf[zs].reshape(tall, depth) for zs in places(u)]
            product = jnp.dot(jnp.concatenate(left, axis=0), right, preferred_element_type=jnp.float32)
            for k, zs in enumerate(places(u)):
                at = pl.ds(pl.multiple_of(zs * tall, tall), tall)
                part[piece, 0, at, :] = product[k * tall: (k + 1) * tall, :LANES]
                part[piece, 1, at, :] = product[k * tall: (k + 1) * tall, LANES:]
            return carry

        lax.fori_loop(0, count, body, 0)

    def toward(me, n, t, d):
        if t is None:
            return me
        return lax.rem(me + (n // 2 - t if d == 0 else n // 2 + t), n)

    def rows_at(piece, h, at_z, at_y):
        return part[piece, h, pl.ds(pl.multiple_of((at_z * ny + at_y) * CHUNK, CHUNK), CHUNK), :]

    def y1_own(v, t, d, s, p, h):
        where = places(v)
        at_z = where[0] if len(where) == 1 else jnp.where(s == 0, where[0], where[1])
        return rows_at(p, h, at_z, toward(y, ny, t, d))

    def z1_own(v, t, d, s, p, h):
        return rows_at(NY + p, h, toward(z, nz, t, d), s)

    def z2_own(v, t, d, s, p, h):
        return qy[nz - 1 if t is None else 0 if t == 0 else 2 * t - 1 + d, p, h]

    def y2_own(v, t, d, s, p, h):
        return qz[toward(y, ny, t, d), p, h]

    bufs = [ring_bufs[5 * k: 5 * k + 5] for k in range(4)]
    y1 = Ring("layer", ny, [len(places(u)) for u in range(half + 1)], Y_GROUPS, y1_own, bufs[0])
    z2 = Ring("perm", nz, [1], Y_GROUPS, z2_own, bufs[1])
    z1 = Ring("perm", nz, [ny], Z_GROUPS, z1_own, bufs[2])
    y2 = Ring("layer", ny, [1], Z_ALL, y2_own, bufs[3])

    def keep_y(u):
        def store(s, p, h, value):
            qy[max(2 * u - 1, 0) + s, p, h] = value
        return store

    def keep_z(s, p, h, value):
        qz[s, p, h] = value

    def write(base):
        def store(s, p, h, value):
            out[:, pl.ds(pl.multiple_of((base + p) * PIECE + h * LANES, LANES), LANES)] = value
        return store

    def brought():
        for k in range(half):
            mine, remote, here = block(k)

            @pl.when(jnp.logical_not(mine))
            def _(remote=remote):
                remote.wait_send()

    def spread_left(u):
        if u > half:
            return

        @pl.when(active)
        def _():
            for zs in places(u):
                for k in range(1, nx):
                    along_x(zs, k).wait_send()
                across(zs).wait_send()

    spread(0)
    spread(1)
    spread(2)
    spread(3)
    spread(4)
    collect(0)
    for i in range(half + 3):
        if i <= half:
            spread(i + 5)
            collect(i + 1)
            arrive(i)
            for g, (first, count) in enumerate(Y_GROUPS):
                multiply(i, first, count)
                y1.send(i, 0, g)
        if i == 1:
            brought()
        if i >= 1:
            spread_left(i - 1)
            y1.drain(2 * len(Y_GROUPS))
            z2.drain(len(Y_GROUPS))
            z1.drain(len(Z_GROUPS))
        if 1 <= i <= half + 1:
            for g in range(len(Y_GROUPS)):
                y1.send(i - 1, 1, g)
        if i <= half:
            for g, (first, count) in enumerate(Z_GROUPS):
                multiply(i, NY + first, count)
                if i < half:
                    z1.send(0, i, g)
                else:
                    z1.final(0, g, keep_z)
        if i == half:
            y2.send(0, 0, 0)
        if i == half + 1:
            y2.send(0, 1, 0)
        if i == half + 2:
            y2.final(0, 0, write(NY))
        if i >= 2:
            u = i - 2
            for g in range(len(Y_GROUPS)):
                y1.final(u, g, keep_y(u))
                if u < half:
                    z2.send(0, u, g)
                else:
                    z2.final(0, g, write(0))

    for ring in (y1, z2, z1, y2):
        ring.drain()


def solution(mesh):
    ny, nz, nx = mesh.shape["layer"], mesh.shape["perm"], mesh.shape["owner"] // 2

    def local(amplitudes, integrals, contract_irrep, output_irrep, occ_energy, virt_energy):
        rows = amplitudes.shape[0]
        depth, width = integrals.shape
        dma = pltpu.SemaphoreType.DMA
        rings = []
        for n, turns, slots, pieces, groups in (
            (ny, nz // 2 + 1, 2, NY, len(Y_GROUPS)),
            (nz, 1, 1, NY, len(Y_GROUPS)),
            (nz, 1, ny, NZ, len(Z_GROUPS)),
            (ny, 1, 1, NZ, len(Z_ALL)),
        ):
            rings += [pltpu.VMEM((turns, n // 2, 2, slots, pieces, 2, CHUNK, LANES), jnp.int16)] * 2
            rings += [pltpu.VMEM((turns, n // 2, 2, slots, pieces, 1, LANES), jnp.float32)] * 2
            rings += [dma((4, turns, n // 2, 2, groups))]
        asems = (
            dma((nz // 2,)), dma((nz,)),
            dma((nz, nx)), dma((nz, nx)),
            dma((nz,)), dma((nz,)),
            dma((depth // BW,)),
        )
        ladder = pl.pallas_call(
            functools.partial(kernel, ny, nz, nx),
            out_shape=jax.ShapeDtypeStruct((rows, width), jnp.float32),
            in_specs=[pl.BlockSpec(memory_space=pltpu.SMEM)] * 2 + [pl.BlockSpec(memory_space=pl.ANY)] * 2,
            out_specs=pl.BlockSpec(memory_space=pltpu.VMEM),
            scratch_shapes=[
                pltpu.VMEM((nz, ny, rows, depth), jnp.bfloat16),
                pltpu.VMEM((depth, width), jnp.bfloat16),
                pltpu.VMEM((NY + NZ, 2, ny * nz * CHUNK, LANES), jnp.float32),
                pltpu.VMEM((nz, NY, 2, CHUNK, LANES), jnp.float32),
                pltpu.VMEM((ny, NZ, 2, CHUNK, LANES), jnp.float32),
                asems,
            ] + rings,
            compiler_params=pltpu.CompilerParams(
                collective_id=0, has_side_effects=True, vmem_limit_bytes=56 * 2**20
            ),
            cost_estimate=pl.CostEstimate(
                flops=2 * ny * nz * rows * depth * width, bytes_accessed=2 * depth * width, transcendentals=0
            ),
        )(contract_irrep, output_irrep, amplitudes, integrals)
        return ladder / (virt_energy[None, :] - occ_energy[:, None])

    return jax.shard_map(
        local,
        mesh=mesh,
        in_specs=(
            P(("layer", "perm"), "owner"),
            P(("layer", "perm"), "owner"),
            P(),
            P(),
            P(("layer", "perm")),
            P("owner"),
        ),
        out_specs=P(("layer", "perm"), "owner"),
        check_vma=False,
    )
```

```python
import functools

import jax
import jax.numpy as jnp
from jax import lax
from jax.experimental import pallas as pl
from jax.experimental.pallas import tpu as pltpu
from jax.sharding import PartitionSpec as P

BW = 128
LANES = 128
CHUNK = 32
PIECE = 256
TOP = 32767.0
MESH = pl.DeviceIdType.MESH

Y_GROUPS = ((0, 3), (3, 2))
Z_GROUPS = ((0, 1), (1, 1), (2, 1))
Z_ALL = ((0, 3),)
NY, NZ = 5, 3


class Ring:
    def __init__(self, axis, n, slots, groups, own, bufs):
        self.axis, self.n, self.slots, self.groups, self.own = axis, n, slots, groups, own
        self.sq, self.rq, self.ss, self.rs, self.sems = bufs
        self.me = lax.axis_index(axis)
        self.started = []

    def copies(self, v, t, d, g):
        where = {self.axis: lax.rem(self.me + (1 if d == 0 else self.n - 1), self.n)}
        first, count = self.groups[g]
        rows, pieces = pl.ds(0, self.slots[v]), pl.ds(first, count)
        at = (v, t, d, rows, pieces, d) if t == 0 else (v, t, d, rows, pieces)
        scales = (v, t, d, rows, pieces)
        return [
            pltpu.make_async_remote_copy(
                src_ref=self.sq.at[at],
                dst_ref=self.rq.at[at],
                send_sem=self.sems.at[0, v, t, d, g],
                recv_sem=self.sems.at[1, v, t, d, g],
                device_id=where,
                device_id_type=MESH,
            ),
            pltpu.make_async_remote_copy(
                src_ref=self.ss.at[scales],
                dst_ref=self.rs.at[scales],
                send_sem=self.sems.at[2, v, t, d, g],
                recv_sem=self.sems.at[3, v, t, d, g],
                device_id=where,
                device_id_type=MESH,
            ),
        ]

    def each(self, v, g, body):
        first, count = self.groups[g]
        total = self.slots[v] * count

        def step(k, carry):
            body(k // count, first + lax.rem(k, count))
            return carry

        lax.fori_loop(0, total, step, 0, unroll=next(w for w in (4, 5, 3, 2, 1) if total % w == 0))

    def decode(self, v, t, d, s, p, h):
        return self.rq[v, t, d, s, p, h].astype(jnp.int32).astype(jnp.float32) * self.rs[v, t, d, s, p]

    def wait(self, v, t, d, g):
        for copy in self.copies(v, t, d, g):
            copy.wait_recv()

    def send(self, v, t, g):
        for d in range(2):
            if t > 0:
                self.wait(v, t - 1, d, g)

            def body(s, p, d=d):
                halves = (d,) if t == 0 else (0, 1)
                values = []
                for h in halves:
                    value = self.own(v, t, d, s, p, h)
                    if t > 1 or (t == 1 and h == d):
                        value = value + self.decode(v, t - 1, d, s, p, h)
                    values.append(value)
                most = jnp.max(functools.reduce(jnp.maximum, [jnp.abs(u) for u in values]), axis=0, keepdims=True)
                scale = jnp.maximum(most, 1e-30) * (1.0 / TOP)
                factor = 1.0 / scale
                self.ss[v, t, d, s, p] = scale
                for h, value in zip(halves, values):
                    self.sq[v, t, d, s, p, h] = jnp.round(value * factor).astype(jnp.int32).astype(jnp.int16)

            self.each(v, g, body)
            for copy in self.copies(v, t, d, g):
                copy.start()
        self.started.append((v, t, g))

    def final(self, v, g, store):
        last = self.n // 2 - 1
        for d in range(2):
            self.wait(v, last, d, g)

        def body(s, p):
            for h in range(2):
                total = self.own(v, None, None, s, p, h) + self.decode(v, last, 0, s, p, h)
                store(s, p, h, total + self.decode(v, last, 1, s, p, h))

        self.each(v, g, body)

    def drain(self, keep=0):
        count = max(len(self.started) - keep, 0)
        for v, t, g in self.started[:count]:
            for d in range(2):
                for copy in self.copies(v, t, d, g):
                    copy.wait_send()
        self.started = self.started[count:]


def kernel(ny, nz, nx, cirr, oirr, amp, integ, out, abuf, im, part, qy, qz, asems, *ring_bufs):
    y, z, o = lax.axis_index("layer"), lax.axis_index("perm"), lax.axis_index("owner")
    x, c = o // 2, lax.rem(o, 2)
    depth, width = im.shape
    half = nz // 2
    a_send, a_recv, x_send, x_recv, b_send, b_recv, i_sem = asems
    active = c == z // half
    sibling = {"owner": o + 1 - 2 * c}

    def row_of(column, zs, at_z):
        return lax.rem(column + 4 * nx - zs - at_z, nx)

    barrier = pltpu.get_barrier_semaphore()

    def greet(where):
        pl.semaphore_signal(barrier, inc=1, device_id=where, device_id_type=MESH)

    for zs in range(nz):
        ys = row_of(x, zs, z)

        @pl.when(active & jnp.logical_not((x == y) & (ys == y) & (z == zs)))
        def _(zs=zs, ys=ys):
            greet({"owner": 2 * y + c, "layer": ys, "perm": jnp.int32(zs)})

    for k in (1, nz - 1):
        greet({"perm": lax.rem(z + k, nz)})
    for k in (1, ny - 1):
        greet({"layer": lax.rem(y + k, ny)})
    for k in range(1, nx):
        greet({"owner": lax.rem(o + 2 * k, 2 * nx)})
    greet(sibling)

    load = [
        pltpu.make_async_copy(integ.at[pl.ds(k * BW, BW)], im.at[pl.ds(k * BW, BW)], i_sem.at[k])
        for k in range(depth // BW)
    ]
    for copy in load:
        copy.start()

    orders = (((0, 1, 2, 3), (1, 0, 2, 3), (2, 1, 3, 0), (3, 2, 1, 0)), ((3, 2, 1, 0), (3, 0, 2, 1), (0, 1, 3, 2), (0, 1, 2, 3)))

    def block(k):
        turn = lax.rem(z, half)
        far, near = [
            functools.reduce(lambda rest, r: jnp.where(turn == r, order[r][k], rest), range(1, half), order[0][k])
            for order in orders
        ]
        j = jnp.where(active, near, far)
        to_z = half * c + j
        column = lax.rem(y + z + to_z, nx)
        mine = (column == x) & (x == y) & (to_z == z)
        source = amp.at[:, pl.ds(pl.multiple_of(j * depth, depth), depth)]
        remote = pltpu.make_async_remote_copy(
            src_ref=source,
            dst_ref=abuf.at[z, y],
            send_sem=a_send.at[k],
            recv_sem=a_recv.at[z],
            device_id={"owner": 2 * column + c, "layer": x, "perm": to_z},
            device_id_type=MESH,
        )
        return mine, remote, pltpu.make_async_copy(source, abuf.at[z, y], a_recv.at[z])

    keeps = active & (x == y) & (lax.rem(y + 2 * z, nx) == x)
    pl.semaphore_wait(barrier, nx + 4 + half - keeps.astype(jnp.int32))
    for k in range(half):
        mine, remote, here = block(k)

        @pl.when(jnp.logical_not(mine))
        def _(remote=remote):
            remote.start()

        @pl.when(mine)
        def _(here=here):
            here.start()

    outer = width // BW
    inner_base = (y * nz + z) * (depth // BW)
    outer_base = o * outer
    for copy in load:
        copy.wait()

    def mask_rows(k, carry):
        row_irrep = cirr[inner_base + k]
        rows = pl.ds(pl.multiple_of(k * BW, BW), BW)
        for b in range(outer):
            cols = pl.ds(b * BW, BW)
            values = im[rows, cols]
            im[rows, cols] = jnp.where(row_irrep == oirr[outer_base + b], values, jnp.zeros_like(values))
        return carry

    lax.fori_loop(0, depth // BW, mask_rows, 0)

    def places(u):
        if u == 0:
            return [lax.rem(z + half, nz)]
        if u == half:
            return [z]
        return [lax.rem(z + half - u, nz), lax.rem(z + half + u, nz)]

    def along_x(zs, k):
        ys = row_of(x, zs, z)
        return pltpu.make_async_remote_copy(
            src_ref=abuf.at[zs, ys],
            dst_ref=abuf.at[zs, ys],
            send_sem=x_send.at[zs, k],
            recv_sem=x_recv.at[zs, k],
            device_id={"owner": lax.rem(o + 2 * k, 2 * nx)},
            device_id_type=MESH,
        )

    def across(zs):
        return pltpu.make_async_remote_copy(
            src_ref=abuf.at[zs],
            dst_ref=abuf.at[zs],
            send_sem=b_send.at[zs],
            recv_sem=b_recv.at[zs],
            device_id=sibling,
            device_id_type=MESH,
        )

    def spread(u):
        if u > half:
            return

        @pl.when(active)
        def _():
            for zs in places(u):
                ys = row_of(x, zs, z)
                pltpu.make_async_copy(abuf.at[zs, ys], abuf.at[zs, ys], a_recv.at[zs]).wait()
                for k in (2, 1, 3):
                    along_x(zs, k).start()

    def collect(u):
        if u > half:
            return

        @pl.when(active)
        def _():
            for zs in places(u):
                for k in range(1, nx):
                    ys = row_of(lax.rem(x + nx - k, nx), zs, z)
                    pltpu.make_async_copy(abuf.at[zs, ys], abuf.at[zs, ys], x_recv.at[zs, k]).wait()
                across(zs).start()

    def arrive(u):
        @pl.when(jnp.logical_not(active))
        def _():
            for zs in places(u):
                across(zs).wait_recv()

    tall = ny * CHUNK

    def multiply(u, first, count):
        def body(k, carry):
            piece = first + k
            right = im[:, pl.ds(pl.multiple_of(piece * PIECE, PIECE), PIECE)]
            left = [abuf[zs].reshape(tall, depth) for zs in places(u)]
            product = jnp.dot(jnp.concatenate(left, axis=0), right, preferred_element_type=jnp.float32)
            for k, zs in enumerate(places(u)):
                at = pl.ds(pl.multiple_of(zs * tall, tall), tall)
                part[piece, 0, at, :] = product[k * tall: (k + 1) * tall, :LANES]
                part[piece, 1, at, :] = product[k * tall: (k + 1) * tall, LANES:]
            return carry

        lax.fori_loop(0, count, body, 0)

    def toward(me, n, t, d):
        if t is None:
            return me
        return lax.rem(me + (n // 2 - t if d == 0 else n // 2 + t), n)

    def rows_at(piece, h, at_z, at_y):
        return part[piece, h, pl.ds(pl.multiple_of((at_z * ny + at_y) * CHUNK, CHUNK), CHUNK), :]

    def y1_own(v, t, d, s, p, h):
        where = places(v)
        at_z = where[0] if len(where) == 1 else jnp.where(s == 0, where[0], where[1])
        return rows_at(p, h, at_z, toward(y, ny, t, d))

    def z1_own(v, t, d, s, p, h):
        return rows_at(NY + p, h, toward(z, nz, t, d), s)

    def z2_own(v, t, d, s, p, h):
        return qy[nz - 1 if t is None else 0 if t == 0 else 2 * t - 1 + d, p, h]

    def y2_own(v, t, d, s, p, h):
        return qz[toward(y, ny, t, d), p, h]

    bufs = [ring_bufs[5 * k: 5 * k + 5] for k in range(4)]
    y1 = Ring("layer", ny, [len(places(u)) for u in range(half + 1)], Y_GROUPS, y1_own, bufs[0])
    z2 = Ring("perm", nz, [1], Y_GROUPS, z2_own, bufs[1])
    z1 = Ring("perm", nz, [ny], Z_GROUPS, z1_own, bufs[2])
    y2 = Ring("layer", ny, [1], Z_ALL, y2_own, bufs[3])

    def keep_y(u):
        def store(s, p, h, value):
            qy[max(2 * u - 1, 0) + s, p, h] = value
        return store

    def keep_z(s, p, h, value):
        qz[s, p, h] = value

    def write(base):
        def store(s, p, h, value):
            out[:, pl.ds(pl.multiple_of((base + p) * PIECE + h * LANES, LANES), LANES)] = value
        return store

    def brought():
        for k in range(half):
            mine, remote, here = block(k)

            @pl.when(jnp.logical_not(mine))
            def _(remote=remote):
                remote.wait_send()

    def spread_left(u):
        if u > half:
            return

        @pl.when(active)
        def _():
            for zs in places(u):
                for k in range(1, nx):
                    along_x(zs, k).wait_send()
                across(zs).wait_send()

    spread(0)
    spread(1)
    spread(2)
    spread(3)
    spread(4)
    collect(0)
    for i in range(half + 3):
        if i <= half:
            spread(i + 5)
            collect(i + 1)
            arrive(i)
            for g, (first, count) in enumerate(Y_GROUPS):
                multiply(i, first, count)
                y1.send(i, 0, g)
        if i == 1:
            brought()
        if i >= 1:
            spread_left(i - 1)
            y1.drain(2 * len(Y_GROUPS))
            z2.drain(len(Y_GROUPS))
            z1.drain(len(Z_GROUPS))
        if 1 <= i <= half + 1:
            for g in range(len(Y_GROUPS)):
                y1.send(i - 1, 1, g)
        if i >= 2:
            u = i - 2
            for g in range(len(Y_GROUPS)):
                y1.final(u, g, keep_y(u))
                if u < half:
                    z2.send(0, u, g)
                else:
                    z2.final(0, g, write(0))
        if i <= half:
            for g, (first, count) in enumerate(Z_GROUPS):
                multiply(i, NY + first, count)
                if i < half:
                    z1.send(0, i, g)
                else:
                    z1.final(0, g, keep_z)
        if i == half:
            y2.send(0, 0, 0)
        if i == half + 1:
            y2.send(0, 1, 0)
        if i == half + 2:
            y2.final(0, 0, write(NY))

    for ring in (y1, z2, z1, y2):
        ring.drain()


def solution(mesh):
    ny, nz, nx = mesh.shape["layer"], mesh.shape["perm"], mesh.shape["owner"] // 2

    def local(amplitudes, integrals, contract_irrep, output_irrep, occ_energy, virt_energy):
        rows = amplitudes.shape[0]
        depth, width = integrals.shape
        dma = pltpu.SemaphoreType.DMA
        rings = []
        for n, turns, slots, pieces, groups in (
            (ny, nz // 2 + 1, 2, NY, len(Y_GROUPS)),
            (nz, 1, 1, NY, len(Y_GROUPS)),
            (nz, 1, ny, NZ, len(Z_GROUPS)),
            (ny, 1, 1, NZ, len(Z_ALL)),
        ):
            rings += [pltpu.VMEM((turns, n // 2, 2, slots, pieces, 2, CHUNK, LANES), jnp.int16)] * 2
            rings += [pltpu.VMEM((turns, n // 2, 2, slots, pieces, 1, LANES), jnp.float32)] * 2
            rings += [dma((4, turns, n // 2, 2, groups))]
        asems = (
            dma((nz // 2,)), dma((nz,)),
            dma((nz, nx)), dma((nz, nx)),
            dma((nz,)), dma((nz,)),
            dma((depth // BW,)),
        )
        ladder = pl.pallas_call(
            functools.partial(kernel, ny, nz, nx),
            out_shape=jax.ShapeDtypeStruct((rows, width), jnp.float32),
            in_specs=[pl.BlockSpec(memory_space=pltpu.SMEM)] * 2 + [pl.BlockSpec(memory_space=pl.ANY)] * 2,
            out_specs=pl.BlockSpec(memory_space=pltpu.VMEM),
            scratch_shapes=[
                pltpu.VMEM((nz, ny, rows, depth), jnp.bfloat16),
                pltpu.VMEM((depth, width), jnp.bfloat16),
                pltpu.VMEM((NY + NZ, 2, ny * nz * CHUNK, LANES), jnp.float32),
                pltpu.VMEM((nz, NY, 2, CHUNK, LANES), jnp.float32),
                pltpu.VMEM((ny, NZ, 2, CHUNK, LANES), jnp.float32),
                asems,
            ] + rings,
            compiler_params=pltpu.CompilerParams(
                collective_id=0, has_side_effects=True, vmem_limit_bytes=56 * 2**20
            ),
            cost_estimate=pl.CostEstimate(
                flops=2 * ny * nz * rows * depth * width, bytes_accessed=2 * depth * width, transcendentals=0
            ),
        )(contract_irrep, output_irrep, amplitudes, integrals)
        return ladder / (virt_energy[None, :] - occ_energy[:, None])

    return jax.shard_map(
        local,
        mesh=mesh,
        in_specs=(
            P(("layer", "perm"), "owner"),
            P(("layer", "perm"), "owner"),
            P(),
            P(),
            P(("layer", "perm")),
            P("owner"),
        ),
        out_specs=P(("layer", "perm"), "owner"),
        check_vma=False,
    )
```

```python
import functools

import jax
import jax.numpy as jnp
from jax import lax
from jax.experimental import pallas as pl
from jax.experimental.pallas import tpu as pltpu
from jax.sharding import PartitionSpec as P

BW = 128
LANES = 128
CHUNK = 32
PIECE = 256
TOP = 32767.0
MESH = pl.DeviceIdType.MESH

Y_GROUPS = ((0, 3), (3, 2))
Z_GROUPS = ((0, 1), (1, 1), (2, 1))
Z_ALL = ((0, 3),)
NY, NZ = 5, 3


class Ring:
    def __init__(self, axis, n, slots, groups, own, bufs):
        self.axis, self.n, self.slots, self.groups, self.own = axis, n, slots, groups, own
        self.sq, self.rq, self.ss, self.rs, self.sems = bufs
        self.me = lax.axis_index(axis)
        self.started = []

    def copies(self, v, t, d, g):
        where = {self.axis: lax.rem(self.me + (1 if d == 0 else self.n - 1), self.n)}
        first, count = self.groups[g]
        rows, pieces = pl.ds(0, self.slots[v]), pl.ds(first, count)
        at = (v, t, d, rows, pieces, d) if t == 0 else (v, t, d, rows, pieces)
        scales = (v, t, d, rows, pieces)
        return [
            pltpu.make_async_remote_copy(
                src_ref=self.sq.at[at],
                dst_ref=self.rq.at[at],
                send_sem=self.sems.at[0, v, t, d, g],
                recv_sem=self.sems.at[1, v, t, d, g],
                device_id=where,
                device_id_type=MESH,
            ),
            pltpu.make_async_remote_copy(
                src_ref=self.ss.at[scales],
                dst_ref=self.rs.at[scales],
                send_sem=self.sems.at[2, v, t, d, g],
                recv_sem=self.sems.at[3, v, t, d, g],
                device_id=where,
                device_id_type=MESH,
            ),
        ]

    def each(self, v, g, body):
        first, count = self.groups[g]
        total = self.slots[v] * count

        def step(k, carry):
            body(k // count, first + lax.rem(k, count))
            return carry

        lax.fori_loop(0, total, step, 0, unroll=next(w for w in (4, 5, 3, 2, 1) if total % w == 0))

    def decode(self, v, t, d, s, p, h):
        return self.rq[v, t, d, s, p, h].astype(jnp.int32).astype(jnp.float32) * self.rs[v, t, d, s, p]

    def wait(self, v, t, d, g):
        for copy in self.copies(v, t, d, g):
            copy.wait_recv()

    def send(self, v, t, g):
        for d in range(2):
            if t > 0:
                self.wait(v, t - 1, d, g)

            def body(s, p, d=d):
                halves = (d,) if t == 0 else (0, 1)
                values = []
                for h in halves:
                    value = self.own(v, t, d, s, p, h)
                    if t > 1 or (t == 1 and h == d):
                        value = value + self.decode(v, t - 1, d, s, p, h)
                    values.append(value)
                most = jnp.max(functools.reduce(jnp.maximum, [jnp.abs(u) for u in values]), axis=0, keepdims=True)
                scale = jnp.maximum(most, 1e-30) * (1.0 / TOP)
                factor = 1.0 / scale
                self.ss[v, t, d, s, p] = scale
                for h, value in zip(halves, values):
                    self.sq[v, t, d, s, p, h] = jnp.round(value * factor).astype(jnp.int32).astype(jnp.int16)

            self.each(v, g, body)
            for copy in self.copies(v, t, d, g):
                copy.start()
        self.started.append((v, t, g))

    def final(self, v, g, store):
        last = self.n // 2 - 1
        for d in range(2):
            self.wait(v, last, d, g)

        def body(s, p):
            for h in range(2):
                total = self.own(v, None, None, s, p, h) + self.decode(v, last, 0, s, p, h)
                store(s, p, h, total + self.decode(v, last, 1, s, p, h))

        self.each(v, g, body)

    def drain(self, keep=0):
        count = max(len(self.started) - keep, 0)
        for v, t, g in self.started[:count]:
            for d in range(2):
                for copy in self.copies(v, t, d, g):
                    copy.wait_send()
        self.started = self.started[count:]


def kernel(ny, nz, nx, cirr, oirr, amp, integ, out, held, abuf, im, part, qy, qz, asems, *ring_bufs):
    y, z, o = lax.axis_index("layer"), lax.axis_index("perm"), lax.axis_index("owner")
    x, c = o // 2, lax.rem(o, 2)
    depth, width = im.shape
    half = nz // 2
    a_send, a_recv, x_send, x_recv, b_send, b_recv, i_sem, h_sem = asems
    active = c == z // half
    sibling = {"owner": o + 1 - 2 * c}

    def row_of(column, zs, at_z):
        return lax.rem(column + 4 * nx - zs - at_z, nx)

    barrier = pltpu.get_barrier_semaphore()

    def greet(where):
        pl.semaphore_signal(barrier, inc=1, device_id=where, device_id_type=MESH)

    for zs in range(nz):
        ys = row_of(x, zs, z)

        @pl.when(active & jnp.logical_not((x == y) & (ys == y) & (z == zs)))
        def _(zs=zs, ys=ys):
            greet({"owner": 2 * y + c, "layer": ys, "perm": jnp.int32(zs)})

    for k in (1, nz - 1):
        greet({"perm": lax.rem(z + k, nz)})
    for k in (1, ny - 1):
        greet({"layer": lax.rem(y + k, ny)})
    for k in range(1, nx):
        greet({"owner": lax.rem(o + 2 * k, 2 * nx)})
    greet(sibling)

    stage = pltpu.make_async_copy(amp, held, h_sem.at[0])
    stage.start()
    load = [
        pltpu.make_async_copy(integ.at[pl.ds(k * BW, BW)], im.at[pl.ds(k * BW, BW)], i_sem.at[k])
        for k in range(depth // BW)
    ]
    for copy in load:
        copy.start()

    orders = (((0, 1, 2, 3), (1, 0, 2, 3), (2, 1, 3, 0), (3, 2, 1, 0)), ((3, 2, 1, 0), (3, 0, 2, 1), (0, 1, 3, 2), (0, 1, 2, 3)))

    def block(k):
        turn = lax.rem(z, half)
        far, near = [
            functools.reduce(lambda rest, r: jnp.where(turn == r, order[r][k], rest), range(1, half), order[0][k])
            for order in orders
        ]
        j = jnp.where(active, near, far)
        to_z = half * c + j
        column = lax.rem(y + z + to_z, nx)
        mine = (column == x) & (x == y) & (to_z == z)
        source = held.at[:, pl.ds(pl.multiple_of(j * depth, depth), depth)]
        remote = pltpu.make_async_remote_copy(
            src_ref=source,
            dst_ref=abuf.at[z, y],
            send_sem=a_send.at[k],
            recv_sem=a_recv.at[z],
            device_id={"owner": 2 * column + c, "layer": x, "perm": to_z},
            device_id_type=MESH,
        )
        return mine, remote, pltpu.make_async_copy(source, abuf.at[z, y], a_recv.at[z])

    keeps = active & (x == y) & (lax.rem(y + 2 * z, nx) == x)
    stage.wait()
    pl.semaphore_wait(barrier, nx + 4 + half - keeps.astype(jnp.int32))
    for k in range(half):
        mine, remote, here = block(k)

        @pl.when(jnp.logical_not(mine))
        def _(remote=remote):
            remote.start()

        @pl.when(mine)
        def _(here=here):
            here.start()

    outer = width // BW
    inner_base = (y * nz + z) * (depth // BW)
    outer_base = o * outer
    for copy in load:
        copy.wait()

    def mask_rows(k, carry):
        row_irrep = cirr[inner_base + k]
        rows = pl.ds(pl.multiple_of(k * BW, BW), BW)
        for b in range(outer):
            cols = pl.ds(b * BW, BW)
            values = im[rows, cols]
            im[rows, cols] = jnp.where(row_irrep == oirr[outer_base + b], values, jnp.zeros_like(values))
        return carry

    lax.fori_loop(0, depth // BW, mask_rows, 0)

    def places(u):
        if u == 0:
            return [lax.rem(z + half, nz)]
        if u == half:
            return [z]
        return [lax.rem(z + half - u, nz), lax.rem(z + half + u, nz)]

    def along_x(zs, k):
        ys = row_of(x, zs, z)
        return pltpu.make_async_remote_copy(
            src_ref=abuf.at[zs, ys],
            dst_ref=abuf.at[zs, ys],
            send_sem=x_send.at[zs, k],
            recv_sem=x_recv.at[zs, k],
            device_id={"owner": lax.rem(o + 2 * k, 2 * nx)},
            device_id_type=MESH,
        )

    def across(zs):
        return pltpu.make_async_remote_copy(
            src_ref=abuf.at[zs],
            dst_ref=abuf.at[zs],
            send_sem=b_send.at[zs],
            recv_sem=b_recv.at[zs],
            device_id=sibling,
            device_id_type=MESH,
        )

    def spread(u):
        if u > half:
            return

        @pl.when(active)
        def _():
            for zs in places(u):
                ys = row_of(x, zs, z)
                pltpu.make_async_copy(abuf.at[zs, ys], abuf.at[zs, ys], a_recv.at[zs]).wait()
                for k in (2, 1, 3):
                    along_x(zs, k).start()

    def collect(u):
        if u > half:
            return

        @pl.when(active)
        def _():
            for zs in places(u):
                for k in range(1, nx):
                    ys = row_of(lax.rem(x + nx - k, nx), zs, z)
                    pltpu.make_async_copy(abuf.at[zs, ys], abuf.at[zs, ys], x_recv.at[zs, k]).wait()
                across(zs).start()

    def arrive(u):
        @pl.when(jnp.logical_not(active))
        def _():
            for zs in places(u):
                across(zs).wait_recv()

    tall = ny * CHUNK

    def multiply(u, first, count):
        def body(k, carry):
            piece = first + k
            right = im[:, pl.ds(pl.multiple_of(piece * PIECE, PIECE), PIECE)]
            left = [abuf[zs].reshape(tall, depth) for zs in places(u)]
            product = jnp.dot(jnp.concatenate(left, axis=0), right, preferred_element_type=jnp.float32)
            for k, zs in enumerate(places(u)):
                at = pl.ds(pl.multiple_of(zs * tall, tall), tall)
                part[piece, 0, at, :] = product[k * tall: (k + 1) * tall, :LANES]
                part[piece, 1, at, :] = product[k * tall: (k + 1) * tall, LANES:]
            return carry

        lax.fori_loop(0, count, body, 0)

    def toward(me, n, t, d):
        if t is None:
            return me
        return lax.rem(me + (n // 2 - t if d == 0 else n // 2 + t), n)

    def rows_at(piece, h, at_z, at_y):
        return part[piece, h, pl.ds(pl.multiple_of((at_z * ny + at_y) * CHUNK, CHUNK), CHUNK), :]

    def y1_own(v, t, d, s, p, h):
        where = places(v)
        at_z = where[0] if len(where) == 1 else jnp.where(s == 0, where[0], where[1])
        return rows_at(p, h, at_z, toward(y, ny, t, d))

    def z1_own(v, t, d, s, p, h):
        return rows_at(NY + p, h, toward(z, nz, t, d), s)

    def z2_own(v, t, d, s, p, h):
        return qy[nz - 1 if t is None else 0 if t == 0 else 2 * t - 1 + d, p, h]

    def y2_own(v, t, d, s, p, h):
        return qz[toward(y, ny, t, d), p, h]

    bufs = [ring_bufs[5 * k: 5 * k + 5] for k in range(4)]
    y1 = Ring("layer", ny, [len(places(u)) for u in range(half + 1)], Y_GROUPS, y1_own, bufs[0])
    z2 = Ring("perm", nz, [1], Y_GROUPS, z2_own, bufs[1])
    z1 = Ring("perm", nz, [ny], Z_GROUPS, z1_own, bufs[2])
    y2 = Ring("layer", ny, [1], Z_ALL, y2_own, bufs[3])

    def keep_y(u):
        def store(s, p, h, value):
            qy[max(2 * u - 1, 0) + s, p, h] = value
        return store

    def keep_z(s, p, h, value):
        qz[s, p, h] = value

    def write(base):
        def store(s, p, h, value):
            out[:, pl.ds(pl.multiple_of((base + p) * PIECE + h * LANES, LANES), LANES)] = value
        return store

    def brought():
        for k in range(half):
            mine, remote, here = block(k)

            @pl.when(jnp.logical_not(mine))
            def _(remote=remote):
                remote.wait_send()

    def spread_left(u):
        if u > half:
            return

        @pl.when(active)
        def _():
            for zs in places(u):
                for k in range(1, nx):
                    along_x(zs, k).wait_send()
                across(zs).wait_send()

    spread(0)
    spread(1)
    spread(2)
    spread(3)
    spread(4)
    collect(0)
    for i in range(half + 3):
        if i <= half:
            spread(i + 5)
            collect(i + 1)
            arrive(i)
            for g, (first, count) in enumerate(Y_GROUPS):
                multiply(i, first, count)
                y1.send(i, 0, g)
        if i == 1:
            brought()
        if i >= 1:
            spread_left(i - 1)
            y1.drain(2 * len(Y_GROUPS))
            z2.drain(len(Y_GROUPS))
            z1.drain(len(Z_GROUPS))
        if 1 <= i <= half + 1:
            for g in range(len(Y_GROUPS)):
                y1.send(i - 1, 1, g)
        if i >= 2:
            u = i - 2
            for g in range(len(Y_GROUPS)):
                y1.final(u, g, keep_y(u))
                if u < half:
                    z2.send(0, u, g)
                else:
                    z2.final(0, g, write(0))
        if i <= half:
            for g, (first, count) in enumerate(Z_GROUPS):
                multiply(i, NY + first, count)
                if i < half:
                    z1.send(0, i, g)
                else:
                    z1.final(0, g, keep_z)
        if i == half:
            y2.send(0, 0, 0)
        if i == half + 1:
            y2.send(0, 1, 0)
        if i == half + 2:
            y2.final(0, 0, write(NY))

    for ring in (y1, z2, z1, y2):
        ring.drain()


def solution(mesh):
    ny, nz, nx = mesh.shape["layer"], mesh.shape["perm"], mesh.shape["owner"] // 2

    def local(amplitudes, integrals, contract_irrep, output_irrep, occ_energy, virt_energy):
        rows = amplitudes.shape[0]
        depth, width = integrals.shape
        dma = pltpu.SemaphoreType.DMA
        rings = []
        for n, turns, slots, pieces, groups in (
            (ny, nz // 2 + 1, 2, NY, len(Y_GROUPS)),
            (nz, 1, 1, NY, len(Y_GROUPS)),
            (nz, 1, ny, NZ, len(Z_GROUPS)),
            (ny, 1, 1, NZ, len(Z_ALL)),
        ):
            rings += [pltpu.VMEM((turns, n // 2, 2, slots, pieces, 2, CHUNK, LANES), jnp.int16)] * 2
            rings += [pltpu.VMEM((turns, n // 2, 2, slots, pieces, 1, LANES), jnp.float32)] * 2
            rings += [dma((4, turns, n // 2, 2, groups))]
        asems = (
            dma((nz // 2,)), dma((nz,)),
            dma((nz, nx)), dma((nz, nx)),
            dma((nz,)), dma((nz,)),
            dma((depth // BW,)),
            dma((1,)),
        )
        ladder = pl.pallas_call(
            functools.partial(kernel, ny, nz, nx),
            out_shape=jax.ShapeDtypeStruct((rows, width), jnp.float32),
            in_specs=[pl.BlockSpec(memory_space=pltpu.SMEM)] * 2 + [pl.BlockSpec(memory_space=pl.ANY)] * 2,
            out_specs=pl.BlockSpec(memory_space=pltpu.VMEM),
            scratch_shapes=[
                pltpu.VMEM(amplitudes.shape, jnp.bfloat16),
                pltpu.VMEM((nz, ny, rows, depth), jnp.bfloat16),
                pltpu.VMEM((depth, width), jnp.bfloat16),
                pltpu.VMEM((NY + NZ, 2, ny * nz * CHUNK, LANES), jnp.float32),
                pltpu.VMEM((nz, NY, 2, CHUNK, LANES), jnp.float32),
                pltpu.VMEM((ny, NZ, 2, CHUNK, LANES), jnp.float32),
                asems,
            ] + rings,
            compiler_params=pltpu.CompilerParams(
                collective_id=0, has_side_effects=True, vmem_limit_bytes=56 * 2**20
            ),
            cost_estimate=pl.CostEstimate(
                flops=2 * ny * nz * rows * depth * width, bytes_accessed=2 * depth * width, transcendentals=0
            ),
        )(contract_irrep, output_irrep, amplitudes, integrals)
        return ladder / (virt_energy[None, :] - occ_energy[:, None])

    return jax.shard_map(
        local,
        mesh=mesh,
        in_specs=(
            P(("layer", "perm"), "owner"),
            P(("layer", "perm"), "owner"),
            P(),
            P(),
            P(("layer", "perm")),
            P("owner"),
        ),
        out_specs=P(("layer", "perm"), "owner"),
        check_vma=False,
    )
```
